128 devices in a mesh: seq: 8 (over x, core), head: 16 (over z, y).
Axes of the slice: x: 4, y: 4, z: 4, core: 2. Of those that a mesh axis runs over, the one named last changes fastest.
Arguments:
- tokens: bfloat16 [16384, 2880], P(('seq', 'head')), may hold values from -6 to 6
- grad_out: bfloat16 [16384, 2880], P(('seq', 'head')), may hold values from -2 to 2
- expert_ids: int32 [16384, 4], P(('seq', 'head')), may hold values from 0 to 127, all different within a row; in each aligned block of 128 rows (0 to 127, 128 to 255, ...) at most 5 rows name the same one
- router_logits: float32 [16384, 4], P(('seq', 'head')), may hold values from -8 to 300
- w_gate: bfloat16 [128, 2880, 1440], P(('seq', 'head')), may hold values from -0.109375 to 0.109375
- w_up: bfloat16 [128, 2880, 1440], P(('seq', 'head')), may hold values from -0.109375 to 0.109375
- w_down: bfloat16 [128, 1440, 2880], P(('seq', 'head')), may hold values from -0.15625 to 0.15625
Outputs:
- grad_tokens: bfloat16 [16384, 2880], P(('seq', 'head'))
- grad_logits: float32 [16384, 4], P(('seq', 'head'))
The draws below stay inside these ranges and needn't reach their ends.
Inputs may be any that keep to these rules, and one draw needn't show every extreme that they name: `expert_ids`: each token names 4 different experts. Among the 128 tokens of one device (aligned blocks of rows) no expert is named more than 5 times, a bound that some block reaches.
All inputs are finite; a program needn't handle non-finite values.
Results may differ from the reference program's by a relative error of at most 0.0057.
Values may be sent and summed in bfloat16 or wider, within the bound.
No kernel may reach another device: no remote copies, remote signals or barrier semaphores. Data moves between devices by JAX's collectives and lax.ppermute only.
A program may use at most 128 MiB of HBM per device.

```python
import math
import jax
import jax.numpy as jnp
import numpy as np
from jax import lax

D = 2880
FF = 1440
TOP = 4
TOK_DEV = 128
EXPERTS = 128
TOKENS = 16384
CAP = 5


def draw_router_logits(key, part):
    key = jax.random.fold_in(key, 7)
    first = jax.random.fold_in(key, 0)
    return jnp.clip(2.0 * jax.random.normal(first, (TOKENS, TOP), jnp.float32), -8.0, 8.0)


def block_scale(rng, dims, cuts, smallest, largest):
    def one(dim, shards_of):
        steps = jax.random.uniform(jax.random.fold_in(jax.random.fold_in(rng, 6), dim), (shards_of,), jnp.float32, smallest / len(cuts), largest / len(cuts))
        return jnp.repeat(jnp.exp(steps), dims[dim] // shards_of).reshape((-1,) + (1,) * (len(dims) - dim - 1))

    loudness = one(*cuts[0])
    for cut in cuts[1:]:
        loudness = loudness * one(*cut)
    return loudness


def shared_out(key, own, number, rows, number_of, top, bound, lean):
    order = jax.random.permutation(key, number_of)
    packed, usual = portions_of(number_of, rows * top, bound, lean, True), portions_of(number_of, rows * top, bound, lean, False)
    places = jnp.arange(number_of)

    def named(tallies, offset_by):
        used = int((tallies > 0).sum())
        fixed = max(1, used // 4)
        shifted = fixed + (places - fixed + offset_by * (used - fixed)) % max(1, number_of - fixed)
        return jnp.zeros((number_of,), jnp.int32).at[order[jnp.where(places < fixed, places, shifted)]].set(jnp.asarray(tallies, jnp.int32))

    tallies = jnp.where(number % 4 == 0, named(packed, number // 4), named(usual, number - number // 4 - 1))
    mixed = jax.random.permutation(jax.random.fold_in(own, 3), number_of)
    donor, sink = mixed[0:number_of // 2 * 2:2], mixed[1:number_of // 2 * 2:2]
    slack = jnp.minimum(tallies[donor] - 1, bound - tallies[sink]) // 2
    slack = jnp.where((donor == order[0]) | (sink == order[0]) | (tallies[sink] == 0), 0, jnp.maximum(slack, 0))
    shifted = jax.random.randint(jax.random.fold_in(own, 4), (number_of // 2,), 0, 1 << 20) % (slack + 1)
    tallies = tallies.at[donor].add(-shifted).at[sink].add(shifted)
    members = jnp.searchsorted(jnp.cumsum(tallies), jnp.arange(rows * top), side="right").astype(jnp.int32)
    listing = members.reshape(top, rows).T
    listing = listing[jax.random.permutation(jax.random.fold_in(own, 1), rows)]
    offset_by = jax.random.randint(jax.random.fold_in(own, 2), (rows, 1), 0, top)
    return jnp.take_along_axis(listing, (jnp.arange(top)[None, :] + offset_by) % top, axis=1)


def portions_of(number_of, total, reach, skew, full):
    portions = [(1 << 20) // math.isqrt(standing ** skew) + 1 for standing in range(1, number_of + 1)]
    largest = reach if full else min(reach, max(-(-total // number_of), total * portions[0] // sum(portions)))
    least = 1 if total - largest >= number_of - 1 else 0
    given, spare = [largest] + [least] * (number_of - 1), total - largest - least * (number_of - 1)
    while spare > 0:
        movable = [i for i in range(1, number_of) if given[i] < largest] or [i for i in range(1, number_of) if given[i] < reach]
        whole, left = sum([portions[i] for i in movable]), spare
        for i in movable:
            addition = min(reach - given[i], max(1, left * portions[i] // whole), spare)
            given[i] = given[i] + addition
            spare = spare - addition
    return np.array(given)


def scatter_about(own_key, extent, deviation, bound, shards=(), held_as=jnp.bfloat16):
    entries = jax.random.normal(own_key, extent, jnp.float32) * deviation
    if len(shards) > 0:
        entries = block_scale(own_key, extent, shards, -0.22, 0.18) * entries
    return jnp.clip(entries, min=-bound, max=bound).astype(held_as)


def setup_inputs(seed: int = 0) -> dict:
    streams_of = jax.random.split(jax.random.key(seed), 8)
    tokens = scatter_about(streams_of[0], (TOKENS, D), 1.0, 6.0, ((0, 128),))
    grad_out = scatter_about(streams_of[1], (TOKENS, D), 0.25, 2.0, ((0, 128),))
    expert_ids_keys = jax.random.split(jax.random.fold_in(streams_of[2], 1), TOKENS // TOK_DEV)
    expert_ids_turns = jax.random.permutation(jax.random.fold_in(streams_of[2], 3), TOKENS // TOK_DEV)
    expert_ids = jax.vmap(lambda own, number: shared_out(jax.random.fold_in(streams_of[2], 2), own, number, TOK_DEV, EXPERTS, TOP, CAP, 2))(expert_ids_keys, expert_ids_turns).reshape((TOKENS, TOP))
    router_logits = draw_router_logits(jax.random.fold_in(streams_of[7], 71), 0)
    w_gate = scatter_about(streams_of[4], (EXPERTS, D, FF), D ** -0.5, 0.109375, ((0, 128),))
    w_up = scatter_about(streams_of[5], (EXPERTS, D, FF), D ** -0.5, 0.109375, ((0, 128),))
    w_down = scatter_about(streams_of[6], (EXPERTS, FF, D), FF ** -0.5, 0.15625, ((0, 128),))
    return dict(tokens=tokens, grad_out=grad_out, expert_ids=expert_ids, router_logits=router_logits, w_gate=w_gate, w_up=w_up, w_down=w_down)


swish_scale = 1.702


def expert_math(rows_in, grads_in, gate_w, up_w, down_w):
    gate_val = jnp.dot(rows_in, gate_w, preferred_element_type=jnp.float32)
    up_val = jnp.dot(rows_in, up_w, preferred_element_type=jnp.float32)
    back_val = jnp.dot(grads_in, down_w.T, preferred_element_type=jnp.float32)
    sigmoid_val = jax.nn.sigmoid(swish_scale * gate_val)
    act_val = gate_val * sigmoid_val
    hidden = act_val * (up_val + 1.0)
    pair_score = jnp.sum(back_val * hidden, axis=-1).astype(jnp.bfloat16)
    d_gate = (back_val * (up_val + 1.0) * (sigmoid_val + swish_scale * gate_val * sigmoid_val * (1.0 - sigmoid_val))).astype(jnp.bfloat16)
    d_up = (back_val * act_val).astype(jnp.bfloat16)
    pair_grad = (jnp.dot(d_gate, gate_w.T, preferred_element_type=jnp.float32)
                 + jnp.dot(d_up, up_w.T, preferred_element_type=jnp.float32)).astype(jnp.bfloat16)
    return pair_grad, pair_score


def reference(tokens, grad_out, expert_ids, router_logits, w_gate, w_up, w_down):
    block_count = TOKENS // TOK_DEV
    pair_count = TOKENS * TOP
    flat_ids = expert_ids.reshape(block_count, TOK_DEV * TOP).astype(jnp.int32)
    onehot = (flat_ids[:, :, None] == jnp.arange(EXPERTS, dtype=jnp.int32)[None, None, :]).astype(jnp.int32)
    slot_rank = jnp.sum((jnp.cumsum(onehot, axis=1) - onehot) * onehot, axis=2).astype(jnp.int32)
    block_start = (jnp.arange(block_count, dtype=jnp.int32) * CAP)[:, None]
    slot_index = (flat_ids * (block_count * CAP) + block_start + slot_rank).reshape(pair_count).astype(jnp.int32)
    slot_owner = jnp.full((EXPERTS * block_count * CAP,), pair_count, jnp.int32)
    slot_owner = slot_owner.at[slot_index].set(jnp.arange(pair_count, dtype=jnp.int32))
    owner_table = slot_owner.reshape(EXPERTS, block_count * CAP)
    weights = jax.nn.softmax(router_logits, axis=-1)
    padded_weights = jnp.concatenate([weights.reshape(pair_count), jnp.zeros((1,), weights.dtype)])
    padded_x = jnp.concatenate([tokens, jnp.zeros((1, D), tokens.dtype)], axis=0)
    padded_dy = jnp.concatenate([grad_out, jnp.zeros((1, D), grad_out.dtype)], axis=0)

    def expert_step(accum_grad, expert):
        owners = owner_table[expert]
        source_row = (owners // TOP).astype(jnp.int32)
        pair_grad, pair_score = expert_math(padded_x[source_row], padded_dy[source_row],
                                            w_gate[expert], w_up[expert], w_down[expert])
        scaled = padded_weights[owners][:, None] * pair_grad.astype(padded_weights.dtype)
        accum_grad = accum_grad.at[source_row].add(scaled)
        return accum_grad, pair_score

    start_grad = jnp.zeros((TOKENS + 1, D), padded_weights.dtype)
    accum_grad, score_table = lax.scan(expert_step, start_grad, jnp.arange(EXPERTS, dtype=jnp.int32))
    grad_tokens = accum_grad[:TOKENS].astype(jnp.bfloat16)
    scores = score_table.reshape(EXPERTS * block_count * CAP)[slot_index].reshape(TOKENS, TOP).astype(weights.dtype)
    grad_logits = weights * (scores - jnp.sum(weights * scores, axis=-1, keepdims=True))
    return grad_tokens, grad_logits
```

```python
import jax
import jax.numpy as jnp
from jax import lax
from jax.experimental import pallas as pl
from jax.experimental.pallas import tpu as pltpu
from jax.sharding import PartitionSpec as P

swish_scale = 1.702

D = 2880
FF = 1440
TOP = 4
TOK = 128
EXP = 128
CAP = 5
ROWS = 8
EXTRA = 2944
PIECE = 768
IN_W = EXTRA + PIECE
OUT_W = 1920
TAIL = D - OUT_W
SCORE_AT = 1024
GROUP = 32
PAIRS = GROUP * CAP
GROUPS = TOK // GROUP
F_STEP = 480
MB = 1024 * 1024
bf16 = jnp.bfloat16
f32 = jnp.float32


def iota(shape, dim):
    return lax.broadcasted_iota(jnp.int32, shape, dim)


def as_bf16(mask):
    return jnp.where(mask, 1.0, 0.0).astype(bf16)


def dot_nt(a, b):
    return lax.dot_general(a, b, (((1,), (1,)), ((), ())), preferred_element_type=f32)


def dot_nn(a, b):
    return jnp.dot(a, b, preferred_element_type=f32)


def ranks_of(ids):
    expert = iota((EXP, TOK), 0)
    naming = ids[0:1, :] == expert
    for k in range(1, TOP):
        naming = jnp.logical_or(naming, ids[k : k + 1, :] == expert)
    before = as_bf16(iota((TOK, TOK), 0) < iota((TOK, TOK), 1))
    rank = dot_nn(as_bf16(naming), before)
    return naming, jnp.where(naming, rank, -1.0)


def dispatch_kernel(ids_ref, x_ref, dy_ref, out_ref, both, pieces):
    step = pl.program_id(0)
    rows = GROUP * ROWS

    @pl.when(step == 0)
    def _():
        both[:, 0:TOK] = x_ref[...]
        both[:, TOK : 2 * TOK] = dy_ref[...]
        for c in range(4):
            high = min(PIECE, D - c * PIECE)
            pieces[0:high, c * TOK : (c + 1) * TOK] = dy_ref[c * PIECE : c * PIECE + high, :]
            if high < PIECE:
                pieces[high:PIECE, c * TOK : (c + 1) * TOK] = jnp.zeros((PIECE - high, TOK), bf16)

    _, rank = ranks_of(ids_ref[...])
    spread = as_bf16(iota((rows, EXP), 1) == step * GROUP + (iota((rows, EXP), 0) >> 3))
    slot = dot_nn(spread, rank.astype(bf16)).astype(jnp.int32)
    q = iota((rows, TOK), 0) & 7
    pick_x = as_bf16(jnp.logical_and(slot == q, q < CAP))
    pick_dy = as_bf16(jnp.logical_and(slot == q - CAP, q >= CAP))
    out_ref[:, 0:D] = dot_nt(jnp.concatenate([pick_x, pick_dy], axis=1), both[...]).astype(bf16)
    out_ref[:, D:EXTRA] = jnp.zeros((rows, EXTRA - D), bf16)
    late = slot == 3 + (q >> 2)
    pick = [as_bf16(jnp.logical_and(late, (q & 3) == c)) for c in range(4)]
    out_ref[:, EXTRA:IN_W] = dot_nt(jnp.concatenate(pick, axis=1), pieces[...]).astype(bf16)


def dispatch(ids, x, dy):
    whole = lambda shape: pl.BlockSpec(shape, lambda i: (0, 0))
    return pl.pallas_call(
        dispatch_kernel,
        grid=(GROUPS,),
        out_shape=jax.ShapeDtypeStruct((EXP * ROWS, IN_W), bf16),
        in_specs=[whole((TOP, TOK)), whole((D, TOK)), whole((D, TOK))],
        out_specs=pl.BlockSpec((GROUP * ROWS, IN_W), lambda i: (i, 0)),
        scratch_shapes=[pltpu.VMEM((D, 2 * TOK), bf16), pltpu.VMEM((PIECE, 4 * TOK), bf16)],
        compiler_params=pltpu.CompilerParams(vmem_limit_bytes=40 * MB),
        cost_estimate=pl.CostEstimate(flops=2 * 1024 * 256 * 4400, bytes_accessed=10 * MB, transcendentals=0),
        name="dispatch",
    )(ids, x, dy)


def expert_kernel(wire_ref, gate_ref, up_ref, down_ref, out_ref, x_all, dy_all, total, score):
    step = pl.program_id(0)
    rows = GROUP * ROWS

    @pl.when(step == 0)
    def _():
        r, c = iota((rows, rows), 0), iota((rows, rows), 1)
        main = as_bf16(c == (r & 31) * ROWS + (r >> 5))
        late = as_bf16(c == (r & 31) * ROWS + ((r >> 5) & 1) * 4 + (r >> 6))
        for g in range(GROUPS):
            at, to = g * rows, g * PAIRS
            front = dot_nn(main, wire_ref[at : at + rows, 0:D]).astype(bf16)
            x_all[to : to + PAIRS, :] = front[0:PAIRS]
            dy_all[to : to + 96, :] = front[PAIRS:rows]
            rest = dot_nn(late, wire_ref[at : at + rows, EXTRA:IN_W]).astype(bf16)
            for p in range(4):
                high = min(PIECE, D - p * PIECE)
                dy_all[to + 96 : to + PAIRS, p * PIECE : p * PIECE + high] = rest[p * 64 : (p + 1) * 64, 0:high]

    for h in range(2):
        part = slice(h * 320, (h + 1) * 320)
        gate = dot_nt(x_all[part, :], gate_ref[...])
        up = dot_nt(x_all[part, :], up_ref[...]) + 1.0
        back = dot_nt(dy_all[part, :], down_ref[...])
        sig = jax.nn.sigmoid(swish_scale * gate)
        act = gate * sig
        back_up = back * up
        own = jnp.sum(act * back_up, axis=1, keepdims=True)
        d_gate = (back_up * (sig + swish_scale * act * (1.0 - sig))).astype(bf16)
        d_up = (back * act).astype(bf16)
        grad = dot_nn(d_gate, gate_ref[...]) + dot_nn(d_up, up_ref[...])

        @pl.when(step == 0)
        def _():
            total[part, :] = grad
            score[part, :] = own

        @pl.when(step > 0)
        def _():
            total[part, :] += grad
            score[part, :] += own

    @pl.when(step == pl.num_programs(0) - 1)
    def _():
        r, c = iota((rows, PAIRS), 0), iota((rows, PAIRS), 1)
        q, s = r & 7, c >> 5
        same = (r >> 3) == (c & 31)
        main = as_bf16(jnp.logical_and(same, q == s))
        left = as_bf16(jnp.logical_and(same, jnp.logical_and(q >= CAP, s == 2 * (q - CAP))))
        right = as_bf16(jnp.logical_and(same, jnp.logical_and(q >= CAP, s == 2 * (q - CAP) + 1)))
        last = as_bf16(jnp.logical_and(same, q == 7))
        for g in range(GROUPS):
            at, to = g * rows, g * PAIRS
            pairs = slice(to, to + PAIRS)
            tail = jnp.concatenate([total[pairs, OUT_W:D], jnp.zeros((PAIRS, SCORE_AT - TAIL), f32)], axis=1)
            late = pltpu.roll(tail, SCORE_AT - TAIL, 1).astype(bf16)
            tail = tail.astype(bf16)
            lane, slot = iota((PAIRS, 128), 1), iota((PAIRS, 128), 0) >> 5
            marks = jnp.where(lane == slot, score[pairs, :], 0.0).astype(bf16)
            body = dot_nn(main, total[pairs, 0:OUT_W].astype(bf16))
            early = dot_nn(left, tail)
            late = dot_nn(right, late)
            marks = dot_nn(last, marks)
            out_ref[at : at + rows, 0:896] = (body[:, 0:896] + early[:, 0:896]).astype(bf16)
            out_ref[at : at + rows, 896:1024] = (body[:, 896:1024] + early[:, 896:1024] + late[:, 0:128]).astype(bf16)
            out_ref[at : at + rows, 1024:1152] = (body[:, 1024:1152] + late[:, 128:256] + marks).astype(bf16)
            out_ref[at : at + rows, 1152:OUT_W] = (body[:, 1152:OUT_W] + late[:, 256:1024]).astype(bf16)


def experts(wire, gate_w, up_w, down_w):
    weights = pl.BlockSpec((F_STEP, D), lambda i: (i, 0))
    return pl.pallas_call(
        expert_kernel,
        grid=(FF // F_STEP,),
        out_shape=jax.ShapeDtypeStruct((TOK * ROWS, OUT_W), bf16),
        in_specs=[pl.BlockSpec((TOK * ROWS, IN_W), lambda i: (0, 0)), weights, weights, weights],
        out_specs=pl.BlockSpec((TOK * ROWS, OUT_W), lambda i: (0, 0)),
        scratch_shapes=[
            pltpu.VMEM((GROUPS * PAIRS, D), bf16),
            pltpu.VMEM((GROUPS * PAIRS, D), bf16),
            pltpu.VMEM((GROUPS * PAIRS, D), f32),
            pltpu.VMEM((GROUPS * PAIRS, 1), f32),
        ],
        compiler_params=pltpu.CompilerParams(vmem_limit_bytes=60 * MB),
        cost_estimate=pl.CostEstimate(flops=2 * 640 * 5 * D * FF, bytes_accessed=37 * MB, transcendentals=640 * FF),
        name="experts",
    )(wire, gate_w, up_w, down_w)


def combine_kernel(ids_ref, logits_ref, wire_ref, tokens_ref, logits_out_ref):
    ids = ids_ref[...]
    logits = logits_ref[...]
    scaled = jnp.exp(logits - jnp.max(logits, axis=0, keepdims=True))
    weights = scaled / jnp.sum(scaled, axis=0, keepdims=True)
    naming, rank = ranks_of(ids)
    expert = iota((EXP, TOK), 0)
    spread_w = jnp.zeros((EXP, TOK), f32)
    for k in range(TOP):
        spread_w = spread_w + jnp.where(ids[k : k + 1, :] == expert, weights[k : k + 1, :], 0.0)

    all_rows = TOK * ROWS
    sevenths = as_bf16(iota((EXP, all_rows), 1) == iota((EXP, all_rows), 0) * ROWS + 7)
    marks = dot_nn(sevenths, wire_ref[:, SCORE_AT : SCORE_AT + 128])
    score_of = jnp.zeros((EXP, TOK), f32)
    for s in range(CAP):
        score_of = score_of + jnp.where(rank == float(s), marks[:, s : s + 1], 0.0)
    scores = [
        jnp.sum(jnp.where(ids[k : k + 1, :] == expert, score_of, 0.0), axis=0, keepdims=True) for k in range(TOP)
    ]
    mean = sum(weights[k : k + 1, :] * scores[k] for k in range(TOP))
    for k in range(TOP):
        logits_out_ref[k : k + 1, :] = weights[k : k + 1, :] * (scores[k] - mean)

    by_token = spread_w.T
    high = by_token.astype(bf16)
    low = (by_token - high.astype(f32)).astype(bf16)
    spread = as_bf16(iota((EXP, all_rows), 0) == iota((EXP, all_rows), 1) >> 3)
    wide = dot_nn(jnp.concatenate([high, low, rank.T.astype(bf16)], axis=0), spread)
    slot = wide[2 * TOK : 3 * TOK].astype(jnp.int32)
    q = iota((TOK, all_rows), 1) & 7
    late = q >= CAP

    def picked(mask):
        return [jnp.where(mask, wide[i * TOK : (i + 1) * TOK], 0.0).astype(bf16) for i in range(2)]

    main = picked(slot == q)
    left = picked(jnp.logical_and(late, slot == 2 * (q - CAP)))
    right = picked(jnp.logical_and(late, slot == 2 * (q - CAP) + 1))
    a = dot_nn(jnp.concatenate(main + left, axis=0), wire_ref[:, 0:896])
    b = dot_nn(jnp.concatenate(main + left + right, axis=0), wire_ref[:, 896:1024])
    c = dot_nn(jnp.concatenate(main + right, axis=0), wire_ref[:, 1024:OUT_W])
    pair = lambda v, i: v[2 * i * TOK : (2 * i + 1) * TOK] + v[(2 * i + 1) * TOK : (2 * i + 2) * TOK]
    front = jnp.concatenate([pair(a, 0), pair(b, 0), pair(c, 0)], axis=1)
    early = jnp.concatenate([pair(a, 1), pair(b, 1)], axis=1)
    after = pltpu.roll(jnp.concatenate([pair(b, 2), pair(c, 1)], axis=1), TAIL, 1)
    lane = iota((TOK, SCORE_AT), 1)
    tail = jnp.where(lane < TAIL, early + after, 0.0)
    for j in range(OUT_W // 128):
        tokens_ref[j * 128 : (j + 1) * 128, :] = front[:, j * 128 : (j + 1) * 128].T.astype(bf16)
    for j in range(8):
        high_row = min(128, TAIL - j * 128)
        turned = tail[:, j * 128 : (j + 1) * 128].T.astype(bf16)
        tokens_ref[OUT_W + j * 128 : OUT_W + j * 128 + high_row, :] = turned[0:high_row]


def combine(ids, logits, wire):
    return pl.pallas_call(
        combine_kernel,
        out_shape=(jax.ShapeDtypeStruct((D, TOK), bf16), jax.ShapeDtypeStruct((TOP, TOK), f32)),
        compiler_params=pltpu.CompilerParams(vmem_limit_bytes=40 * MB),
        cost_estimate=pl.CostEstimate(flops=2 * 512 * 1024 * OUT_W, bytes_accessed=5 * MB, transcendentals=512),
        name="combine",
    )(ids, logits, wire)


def exchange(wire):
    rows, width = wire.shape
    cut = wire.reshape(EXP, ROWS, width)
    return lax.all_to_all(cut, ("seq", "head"), split_axis=0, concat_axis=0, tiled=True).reshape(rows, width)


def body(tokens, grad_out, expert_ids, router_logits, w_gate, w_up, w_down):
    ids = expert_ids.T
    there = exchange(dispatch(ids, tokens.T, grad_out.T))
    back = exchange(experts(there, w_gate[0].T, w_up[0].T, w_down[0]))
    grad_tokens, grad_logits = combine(ids, router_logits.T, back)
    return grad_tokens.T, grad_logits.T


def solution(mesh):
    rows = P(("seq", "head"), None)
    slabs = P(("seq", "head"), None, None)
    return jax.shard_map(
        body,
        mesh=mesh,
        in_specs=(rows, rows, rows, rows, slabs, slabs, slabs),
        out_specs=(rows, rows),
        check_vma=False,
    )
```

```python
import jax
import jax.numpy as jnp
from jax import lax
from jax.experimental import pallas as pl
from jax.experimental.pallas import tpu as pltpu
from jax.sharding import PartitionSpec as P

swish_scale = 1.702

D = 2880
FF = 1440
TOP = 4
TOK = 128
EXP = 128
CAP = 5
ROWS = 8
EXTRA = 2944
PIECE = 768
IN_W = EXTRA + PIECE
OUT_W = 1920
TAIL = D - OUT_W
RIGHT = 1024
SCORE_AT = 1280
GROUP = 32
PAIRS = GROUP * CAP
GROUPS = TOK // GROUP
def parts_of(total, width):
    return [(start, min(width, total - start)) for start in range(0, total, width)]


F_PARTS = parts_of(FF, 256)
D_PARTS = parts_of(D, 512)
VMEM_MB = 24
SEND_STEPS, SEND_MB = 2, 24
MB = 1024 * 1024
bf16 = jnp.bfloat16
f32 = jnp.float32


def iota(shape, dim):
    return lax.broadcasted_iota(jnp.int32, shape, dim)


def as_bf16(mask):
    return jnp.where(mask, 1.0, 0.0).astype(bf16)


def dot_nt(a, b):
    return lax.dot_general(a, b, (((1,), (1,)), ((), ())), preferred_element_type=f32)


def dot_nn(a, b):
    return jnp.dot(a, b, preferred_element_type=f32)


def ranks_of(ids):
    expert = iota((EXP, TOK), 0)
    naming = ids[0:1, :] == expert
    for k in range(1, TOP):
        naming = jnp.logical_or(naming, ids[k : k + 1, :] == expert)
    before = as_bf16(iota((TOK, TOK), 0) < iota((TOK, TOK), 1))
    rank = dot_nn(as_bf16(naming), before)
    return naming, jnp.where(naming, rank, -1.0)


def dispatch_kernel(ids_ref, x_ref, dy_ref, weight_hbm, out_ref, weight_ref, both, pieces, sem):
    step = pl.program_id(0)
    rows = EXP // SEND_STEPS * ROWS
    keep = pltpu.make_async_copy(weight_hbm, weight_ref, sem)

    @pl.when(step == 0)
    def _():
        keep.start()
        both[:, 0:TOK] = x_ref[...]
        both[:, TOK : 2 * TOK] = dy_ref[...]
        for c in range(4):
            high = min(PIECE, D - c * PIECE)
            pieces[0:high, c * TOK : (c + 1) * TOK] = dy_ref[c * PIECE : c * PIECE + high, :]
            if high < PIECE:
                pieces[high:PIECE, c * TOK : (c + 1) * TOK] = jnp.zeros((PIECE - high, TOK), bf16)

    _, rank = ranks_of(ids_ref[...])
    spread = as_bf16(iota((rows, EXP), 1) == step * (rows // ROWS) + (iota((rows, EXP), 0) >> 3))
    slot = dot_nn(spread, rank.astype(bf16)).astype(jnp.int32)
    q = iota((rows, TOK), 0) & 7
    pick_x = as_bf16(jnp.logical_and(slot == q, q < CAP))
    pick_dy = as_bf16(jnp.logical_and(slot == q - CAP, q >= CAP))
    out_ref[:, 0:D] = dot_nt(jnp.concatenate([pick_x, pick_dy], axis=1), both[...]).astype(bf16)
    out_ref[:, D:EXTRA] = jnp.zeros((rows, EXTRA - D), bf16)
    late = slot == 3 + (q >> 2)
    pick = [as_bf16(jnp.logical_and(late, (q & 3) == c)) for c in range(4)]
    out_ref[:, EXTRA:IN_W] = dot_nt(jnp.concatenate(pick, axis=1), pieces[...]).astype(bf16)

    @pl.when(step == SEND_STEPS - 1)
    def _():
        keep.wait()


def dispatch(ids, x, dy, weight):
    whole = lambda shape: pl.BlockSpec(shape, lambda i: (0, 0))
    operands = [pltpu.with_memory_space_constraint(v, pltpu.HBM) for v in (ids, x, dy, weight)]
    return pl.pallas_call(
        dispatch_kernel,
        grid=(SEND_STEPS,),
        out_shape=(pltpu.HBM((EXP * ROWS, IN_W), bf16), pltpu.VMEM((FF, D), bf16)),
        in_specs=[whole((TOP, TOK)), whole((D, TOK)), whole((D, TOK)), pl.BlockSpec(memory_space=pl.ANY)],
        out_specs=(
            pl.BlockSpec((EXP * ROWS // SEND_STEPS, IN_W), lambda i: (i, 0)),
            pl.BlockSpec(memory_space=pltpu.VMEM),
        ),
        scratch_shapes=[
            pltpu.VMEM((D, 2 * TOK), bf16),
            pltpu.VMEM((PIECE, 4 * TOK), bf16),
            pltpu.SemaphoreType.DMA,
        ],
        compiler_params=pltpu.CompilerParams(vmem_limit_bytes=SEND_MB * MB),
        cost_estimate=pl.CostEstimate(flops=2 * 1024 * 256 * 4400, bytes_accessed=10 * MB, transcendentals=0),
        name="dispatch",
    )(*operands)


def place(slot, block):
    tail = block - OUT_W // 128
    if tail < 0:
        return slot, block
    if slot % 2 == 0:
        return CAP + slot // 2, tail
    if tail < 7:
        return CAP + slot // 2, RIGHT // 128 + tail
    return 7, RIGHT // 128 + slot // 2


def expert_kernel(wire, gate_w, up_w, down_w, out_ref, x_all, dy_all, d_gate, d_up, wide):
    rows = GROUP * ROWS
    r, c = iota((rows, rows), 0), iota((rows, rows), 1)
    main = as_bf16(c == (r & 31) * ROWS + (r >> 5))
    late = as_bf16(c == (r & 31) * ROWS + ((r >> 5) & 1) * 4 + (r >> 6))
    for g in range(GROUPS):
        to = g * PAIRS
        at = slice(g * rows, (g + 1) * rows)
        front = dot_nn(main, wire[at, 0:D]).astype(bf16)
        x_all[to : to + PAIRS, :] = front[0:PAIRS]
        dy_all[to : to + 96, :] = front[PAIRS:rows]
        rest = dot_nn(late, wire[at, EXTRA:IN_W]).astype(bf16)
        for p in range(4):
            high = min(PIECE, D - p * PIECE)
            dy_all[to + 96 : to + PAIRS, p * PIECE : p * PIECE + high] = rest[p * 64 : (p + 1) * 64, 0:high]

    score = jnp.zeros((GROUPS * PAIRS, 1), f32)
    held = None
    for j in range(len(F_PARTS) + 1):
        fresh = None
        if j < len(F_PARTS):
            start, width = F_PARTS[j]
            units = slice(start, start + width)
            fresh = (
                units,
                dot_nt(x_all[...], gate_w[units, :]),
                dot_nt(x_all[...], up_w[units, :]),
                dot_nt(dy_all[...], down_w[units, :]),
            )
        if held is not None:
            units, gate, up, back = held
            sig = jax.nn.sigmoid(swish_scale * gate)
            act = gate * sig
            back_up = back * (up + 1.0)
            score = score + jnp.sum(act * back_up, axis=1, keepdims=True)
            d_gate[:, units] = (back_up * (sig + swish_scale * act * (1.0 - sig))).astype(bf16)
            d_up[:, units] = (back * act).astype(bf16)
        held = fresh

    half = 2 * rows
    for h in range(2):
        own = slice(2 * h * PAIRS, 2 * (h + 1) * PAIRS)
        for start, width in D_PARTS:
            columns = slice(start, start + width)
            grad = dot_nn(d_gate[own, :], gate_w[:, columns]) + dot_nn(d_up[own, :], up_w[:, columns])
            if width % 128:
                grad = jnp.concatenate([grad, jnp.zeros((2 * PAIRS, 64), f32)], axis=1)
            for g in range(2):
                for s in range(CAP):
                    at = g * PAIRS + s * GROUP
                    for n in range(0, width, 128):
                        q, to = place(s, (start + n) // 128)
                        block = grad[at : at + GROUP, n : n + 128]
                        wide[to, pl.ds(g * rows + q, GROUP, stride=ROWS), :] = block
        for g in range(2):
            for s in range(CAP):
                at = (2 * h + g) * PAIRS + s * GROUP
                wide[SCORE_AT // 128 + s, pl.ds(g * rows + 7, GROUP, stride=ROWS), :] = jnp.broadcast_to(
                    score[at : at + GROUP], (GROUP, 128)
                )
        for n in range(OUT_W // 128):
            out_ref[h * half : (h + 1) * half, n * 128 : (n + 1) * 128] = wide[n].astype(bf16)


def experts(wire, gate_w, up_w, down_w):
    near = pl.BlockSpec(memory_space=pltpu.VMEM)
    operands = [pltpu.with_memory_space_constraint(v, pltpu.VMEM) for v in (wire, gate_w, up_w, down_w)]
    return pl.pallas_call(
        expert_kernel,
        out_shape=pltpu.VMEM((TOK * ROWS, OUT_W), bf16),
        in_specs=[near] * 4,
        out_specs=near,
        scratch_shapes=[
            pltpu.VMEM((GROUPS * PAIRS, D), bf16),
            pltpu.VMEM((GROUPS * PAIRS, D), bf16),
            pltpu.VMEM((GROUPS * PAIRS, FF), bf16),
            pltpu.VMEM((GROUPS * PAIRS, FF), bf16),
            pltpu.VMEM((OUT_W // 128, 2 * GROUP * ROWS, 128), f32),
        ],
        compiler_params=pltpu.CompilerParams(vmem_limit_bytes=VMEM_MB * MB),
        cost_estimate=pl.CostEstimate(flops=2 * 640 * 5 * D * FF, bytes_accessed=37 * MB, transcendentals=640 * FF),
        name="experts",
    )(*operands)


def combine_kernel(ids_ref, logits_ref, wire_ref, tokens_ref, logits_out_ref):
    ids = ids_ref[...]
    logits = logits_ref[...]
    scaled = jnp.exp(logits - jnp.max(logits, axis=0, keepdims=True))
    weights = scaled / jnp.sum(scaled, axis=0, keepdims=True)
    naming, rank = ranks_of(ids)
    expert = iota((EXP, TOK), 0)
    spread_w = jnp.zeros((EXP, TOK), f32)
    for k in range(TOP):
        spread_w = spread_w + jnp.where(ids[k : k + 1, :] == expert, weights[k : k + 1, :], 0.0)

    all_rows = TOK * ROWS
    sevenths = as_bf16(iota((EXP, all_rows), 1) == iota((EXP, all_rows), 0) * ROWS + 7)
    marks = dot_nn(sevenths, wire_ref[:, SCORE_AT:OUT_W])
    score_of = jnp.zeros((EXP, TOK), f32)
    for s in range(CAP):
        score_of = score_of + jnp.where(rank == float(s), marks[:, 128 * s : 128 * s + 1], 0.0)
    scores = [
        jnp.sum(jnp.where(ids[k : k + 1, :] == expert, score_of, 0.0), axis=0, keepdims=True) for k in range(TOP)
    ]
    mean = sum(weights[k : k + 1, :] * scores[k] for k in range(TOP))
    for k in range(TOP):
        logits_out_ref[k : k + 1, :] = weights[k : k + 1, :] * (scores[k] - mean)

    spread = as_bf16(iota((EXP, all_rows), 0) == iota((EXP, all_rows), 1) >> 3)
    wide = dot_nn(jnp.concatenate([spread_w.T, rank.T], axis=0).astype(bf16), spread)
    weight = wide[0:TOK].astype(bf16)
    slot = wide[TOK : 2 * TOK].astype(jnp.int32)
    q = iota((TOK, all_rows), 1) & 7
    late = q >= CAP

    def picked(mask):
        return jnp.where(mask, weight, jnp.zeros((), bf16))

    main = picked(slot == q)
    left = picked(jnp.logical_and(late, slot == 2 * (q - CAP)))
    right = picked(jnp.logical_and(late, slot == 2 * (q - CAP) + 1))
    ends = [
        dot_nn(picked(jnp.logical_and(q == 7, slot == 2 * i + 1)), wire_ref[:, RIGHT + 128 * i : RIGHT + 128 * (i + 1)])
        for i in range(2)
    ]
    a = dot_nn(jnp.concatenate([main, left], axis=0), wire_ref[:, 0:RIGHT])
    b = dot_nn(jnp.concatenate([main, right], axis=0), wire_ref[:, RIGHT:OUT_W])
    front = jnp.concatenate([a[0:TOK], b[0:TOK]], axis=1)
    tail = a[TOK : 2 * TOK] + jnp.concatenate([b[TOK : 2 * TOK], ends[0] + ends[1]], axis=1)
    for j in range(OUT_W // 128):
        tokens_ref[j * 128 : (j + 1) * 128, :] = front[:, j * 128 : (j + 1) * 128].T.astype(bf16)
    for j in range(8):
        high_row = min(128, TAIL - j * 128)
        turned = tail[:, j * 128 : (j + 1) * 128].T.astype(bf16)
        tokens_ref[OUT_W + j * 128 : OUT_W + j * 128 + high_row, :] = turned[0:high_row]


def combine(ids, logits, wire):
    return pl.pallas_call(
        combine_kernel,
        out_shape=(jax.ShapeDtypeStruct((D, TOK), bf16), jax.ShapeDtypeStruct((TOP, TOK), f32)),
        compiler_params=pltpu.CompilerParams(vmem_limit_bytes=20 * MB),
        cost_estimate=pl.CostEstimate(flops=2 * 512 * 1024 * OUT_W, bytes_accessed=5 * MB, transcendentals=512),
        name="combine",
    )(ids, logits, wire)


def exchange(wire):
    rows, width = wire.shape
    cut = wire.reshape(EXP, ROWS, width)
    return lax.all_to_all(cut, ("seq", "head"), split_axis=0, concat_axis=0, tiled=True).reshape(rows, width)


def body(tokens, grad_out, expert_ids, router_logits, w_gate, w_up, w_down):
    ids = expert_ids.T
    sent, down = dispatch(ids, tokens.T, grad_out.T, w_down[0])
    back = exchange(experts(exchange(sent), w_gate[0].T, w_up[0].T, down))
    grad_tokens, grad_logits = combine(ids, router_logits.T, back)
    return grad_tokens.T, grad_logits.T


def solution(mesh):
    rows = P(("seq", "head"), None)
    slabs = P(("seq", "head"), None, None)
    return jax.shard_map(
        body,
        mesh=mesh,
        in_specs=(rows, rows, rows, rows, slabs, slabs, slabs),
        out_specs=(rows, rows),
        check_vma=False,
    )
```

```python
import jax
import jax.numpy as jnp
from jax import lax
from jax.experimental import pallas as pl
from jax.experimental.pallas import tpu as pltpu
from jax.sharding import PartitionSpec as P

swish_scale = 1.702

D = 2880
FF = 1440
TOP = 4
TOK = 128
EXP = 128
CAP = 5
ROWS = 8
EXTRA = 2944
PIECE = 768
IN_W = EXTRA + PIECE
OUT_W = 1920
TAIL = D - OUT_W
RIGHT = 1024
SCORE_AT = 1280
GROUP = 32
PAIRS = GROUP * CAP
GROUPS = TOK // GROUP


def parts_of(total, width):
    return [(start, min(width, total - start)) for start in range(0, total, width)]


F_PARTS = parts_of(FF, 256)
D_PARTS = parts_of(D, 512)
VMEM_MB = 26
P_PARTS = parts_of(D, PIECE)
SEND_STEPS, SEND_MB = 4, 24
MB = 1024 * 1024
bf16 = jnp.bfloat16
f32 = jnp.float32


def iota(shape, dim):
    return lax.broadcasted_iota(jnp.int32, shape, dim)


def as_bf16(mask):
    return jnp.where(mask, 1.0, 0.0).astype(bf16)


def dot_nt(a, b):
    return lax.dot_general(a, b, (((1,), (1,)), ((), ())), preferred_element_type=f32)


def dot_nn(a, b):
    return jnp.dot(a, b, preferred_element_type=f32)


def ranks_of(ids):
    expert = iota((EXP, TOK), 0)
    naming = ids[0:1, :] == expert
    for k in range(1, TOP):
        naming = jnp.logical_or(naming, ids[k : k + 1, :] == expert)
    before = as_bf16(iota((TOK, TOK), 0) < iota((TOK, TOK), 1))
    rank = dot_nn(as_bf16(naming), before)
    return naming, jnp.where(naming, rank, -1.0)


def dispatch_kernel(ids_ref, x_hbm, dy_hbm, out_hbm, both, pieces, parts, in_sem, out_sem):
    sources = [(x_hbm, both.at[:, 0:TOK]), (dy_hbm, both.at[:, TOK : 2 * TOK])]
    for c, (start, width) in enumerate(P_PARTS):
        lanes = slice(c * TOK, (c + 1) * TOK)
        sources.append((dy_hbm.at[start : start + width, :], pieces.at[0:width, lanes]))
        if width < PIECE:
            pieces[width:PIECE, lanes] = jnp.zeros((PIECE - width, TOK), bf16)
    fetches = [pltpu.make_async_copy(source, to, in_sem.at[n]) for n, (source, to) in enumerate(sources)]
    for fetch in fetches:
        fetch.start()

    _, rank = ranks_of(ids_ref[...])
    rank = rank.astype(bf16)
    rows = EXP // SEND_STEPS * ROWS
    q = iota((rows, TOK), 0) & 7
    picks = []
    for n in range(SEND_STEPS):
        spread = as_bf16(iota((rows, EXP), 1) == n * (rows // ROWS) + (iota((rows, EXP), 0) >> 3))
        slot = dot_nn(spread, rank).astype(jnp.int32)
        front = [jnp.logical_and(slot == q, q < CAP), jnp.logical_and(slot == q - CAP, q >= CAP)]
        late = slot == 3 + (q >> 2)
        rest = [jnp.logical_and(late, (q & 3) == c) for c in range(4)]
        picks.append([jnp.concatenate([as_bf16(m) for m in masks], axis=1) for masks in (front, rest)])
        parts[n, :, D:EXTRA] = jnp.zeros((rows, EXTRA - D), bf16)
    for fetch in fetches:
        fetch.wait()
    sends = []
    for n, (front, rest) in enumerate(picks):
        parts[n, :, 0:D] = dot_nt(front, both[...]).astype(bf16)
        parts[n, :, EXTRA:IN_W] = dot_nt(rest, pieces[...]).astype(bf16)
        sends.append(pltpu.make_async_copy(parts.at[n], out_hbm.at[n * rows : (n + 1) * rows, :], out_sem.at[n]))
        sends[n].start()
    for send in sends:
        send.wait()


def dispatch(ids, x, dy):
    anywhere = pl.BlockSpec(memory_space=pl.ANY)
    operands = [pltpu.with_memory_space_constraint(v, pltpu.HBM) for v in (ids, x, dy)]
    return pl.pallas_call(
        dispatch_kernel,
        out_shape=pltpu.HBM((EXP * ROWS, IN_W), bf16),
        in_specs=[pl.BlockSpec(memory_space=pltpu.VMEM), anywhere, anywhere],
        out_specs=anywhere,
        scratch_shapes=[
            pltpu.VMEM((D, 2 * TOK), bf16),
            pltpu.VMEM((PIECE, 4 * TOK), bf16),
            pltpu.VMEM((SEND_STEPS, EXP // SEND_STEPS * ROWS, IN_W), bf16),
            pltpu.SemaphoreType.DMA((2 + len(P_PARTS),)),
            pltpu.SemaphoreType.DMA((SEND_STEPS,)),
        ],
        compiler_params=pltpu.CompilerParams(vmem_limit_bytes=SEND_MB * MB),
        cost_estimate=pl.CostEstimate(flops=8 * 1024 * 256 * 4400, bytes_accessed=40 * MB, transcendentals=0),
        name="dispatch",
    )(*operands)


def place(slot, block):
    tail = block - OUT_W // 128
    if tail < 0:
        return slot, block
    if slot % 2 == 0:
        return CAP + slot // 2, tail
    if tail < 7:
        return CAP + slot // 2, RIGHT // 128 + tail
    return 7, RIGHT // 128 + slot // 2


def expert_kernel(wire, gate_w, up_w, down_w, out_ref, x_all, dy_all, d_gate, d_up, wide):
    rows = GROUP * ROWS
    r, c = iota((rows, rows), 0), iota((rows, rows), 1)
    main = as_bf16(c == (r & 31) * ROWS + (r >> 5))
    late = as_bf16(c == (r & 31) * ROWS + ((r >> 5) & 1) * 4 + (r >> 6))
    for g in range(GROUPS):
        to = g * PAIRS
        at = slice(g * rows, (g + 1) * rows)
        front = dot_nn(main, wire[at, 0:D]).astype(bf16)
        x_all[to : to + PAIRS, :] = front[0:PAIRS]
        dy_all[to : to + 96, :] = front[PAIRS:rows]
        rest = dot_nn(late, wire[at, EXTRA:IN_W]).astype(bf16)
        for p in range(4):
            high = min(PIECE, D - p * PIECE)
            dy_all[to + 96 : to + PAIRS, p * PIECE : p * PIECE + high] = rest[p * 64 : (p + 1) * 64, 0:high]

    score = jnp.zeros((GROUPS * PAIRS, 1), f32)
    held = None
    for j in range(len(F_PARTS) + 1):
        fresh = None
        if j < len(F_PARTS):
            start, width = F_PARTS[j]
            units = slice(start, start + width)
            fresh = (
                units,
                dot_nt(x_all[...], gate_w[units, :]),
                dot_nt(x_all[...], up_w[units, :]),
                dot_nt(dy_all[...], down_w[units, :]),
            )
        if held is not None:
            units, gate, up, back = held
            sig = jax.nn.sigmoid(swish_scale * gate)
            act = gate * sig
            back_up = back * (up + 1.0)
            score = score + jnp.sum(act * back_up, axis=1, keepdims=True)
            d_gate[:, units] = (back_up * (sig + swish_scale * act * (1.0 - sig))).astype(bf16)
            d_up[:, units] = (back * act).astype(bf16)
        held = fresh

    half = 2 * rows
    for h in range(2):
        own = slice(2 * h * PAIRS, 2 * (h + 1) * PAIRS)
        for start, width in D_PARTS:
            columns = slice(start, start + width)
            grad = dot_nn(d_gate[own, :], gate_w[:, columns]) + dot_nn(d_up[own, :], up_w[:, columns])
            if width % 128:
                grad = jnp.concatenate([grad, jnp.zeros((2 * PAIRS, 64), f32)], axis=1)
            for g in range(2):
                for s in range(CAP):
                    at = g * PAIRS + s * GROUP
                    for n in range(0, width, 128):
                        q, to = place(s, (start + n) // 128)
                        block = grad[at : at + GROUP, n : n + 128]
                        wide[to, pl.ds(g * rows + q, GROUP, stride=ROWS), :] = block
        for g in range(2):
            for s in range(CAP):
                at = (2 * h + g) * PAIRS + s * GROUP
                wide[SCORE_AT // 128 + s, pl.ds(g * rows + 7, GROUP, stride=ROWS), :] = jnp.broadcast_to(
                    score[at : at + GROUP], (GROUP, 128)
                )
        for n in range(OUT_W // 128):
            out_ref[h * half : (h + 1) * half, n * 128 : (n + 1) * 128] = wide[n].astype(bf16)


def experts(wire, gate_w, up_w, down_w):
    near = pl.BlockSpec(memory_space=pltpu.VMEM)
    operands = [pltpu.with_memory_space_constraint(v, pltpu.VMEM) for v in (wire, gate_w, up_w, down_w)]
    return pl.pallas_call(
        expert_kernel,
        out_shape=pltpu.VMEM((TOK * ROWS, OUT_W), bf16),
        in_specs=[near] * 4,
        out_specs=near,
        scratch_shapes=[
            pltpu.VMEM((GROUPS * PAIRS, D), bf16),
            pltpu.VMEM((GROUPS * PAIRS, D), bf16),
            pltpu.VMEM((GROUPS * PAIRS, FF), bf16),
            pltpu.VMEM((GROUPS * PAIRS, FF), bf16),
            pltpu.VMEM((OUT_W // 128, 2 * GROUP * ROWS, 128), f32),
        ],
        compiler_params=pltpu.CompilerParams(vmem_limit_bytes=VMEM_MB * MB),
        cost_estimate=pl.CostEstimate(flops=2 * 640 * 5 * D * FF, bytes_accessed=37 * MB, transcendentals=640 * FF),
        name="experts",
    )(*operands)


def combine_kernel(ids_ref, logits_ref, wire_ref, tokens_ref, logits_out_ref):
    ids = ids_ref[...]
    logits = logits_ref[...]
    scaled = jnp.exp(logits - jnp.max(logits, axis=0, keepdims=True))
    weights = scaled / jnp.sum(scaled, axis=0, keepdims=True)
    naming, rank = ranks_of(ids)
    expert = iota((EXP, TOK), 0)
    spread_w = jnp.zeros((EXP, TOK), f32)
    for k in range(TOP):
        spread_w = spread_w + jnp.where(ids[k : k + 1, :] == expert, weights[k : k + 1, :], 0.0)

    all_rows = TOK * ROWS
    sevenths = as_bf16(iota((EXP, all_rows), 1) == iota((EXP, all_rows), 0) * ROWS + 7)
    marks = dot_nn(sevenths, wire_ref[:, SCORE_AT:OUT_W])
    score_of = jnp.zeros((EXP, TOK), f32)
    for s in range(CAP):
        score_of = score_of + jnp.where(rank == float(s), marks[:, 128 * s : 128 * s + 1], 0.0)
    scores = [
        jnp.sum(jnp.where(ids[k : k + 1, :] == expert, score_of, 0.0), axis=0, keepdims=True) for k in range(TOP)
    ]
    mean = sum(weights[k : k + 1, :] * scores[k] for k in range(TOP))
    for k in range(TOP):
        logits_out_ref[k : k + 1, :] = weights[k : k + 1, :] * (scores[k] - mean)

    spread = as_bf16(iota((EXP, all_rows), 0) == iota((EXP, all_rows), 1) >> 3)
    wide = dot_nn(jnp.concatenate([spread_w.T, rank.T], axis=0).astype(bf16), spread)
    weight = wide[0:TOK].astype(bf16)
    slot = wide[TOK : 2 * TOK].astype(jnp.int32)
    q = iota((TOK, all_rows), 1) & 7
    late = q >= CAP

    def picked(mask):
        return jnp.where(mask, weight, jnp.zeros((), bf16))

    main = picked(slot == q)
    left = picked(jnp.logical_and(late, slot == 2 * (q - CAP)))
    right = picked(jnp.logical_and(late, slot == 2 * (q - CAP) + 1))
    ends = [
        dot_nn(picked(jnp.logical_and(q == 7, slot == 2 * i + 1)), wire_ref[:, RIGHT + 128 * i : RIGHT + 128 * (i + 1)])
        for i in range(2)
    ]
    a = dot_nn(jnp.concatenate([main, left], axis=0), wire_ref[:, 0:RIGHT])
    b = dot_nn(jnp.concatenate([main, right], axis=0), wire_ref[:, RIGHT:OUT_W])
    front = jnp.concatenate([a[0:TOK], b[0:TOK]], axis=1)
    tail = a[TOK : 2 * TOK] + jnp.concatenate([b[TOK : 2 * TOK], ends[0] + ends[1]], axis=1)
    for j in range(OUT_W // 128):
        tokens_ref[j * 128 : (j + 1) * 128, :] = front[:, j * 128 : (j + 1) * 128].T.astype(bf16)
    for j in range(8):
        high_row = min(128, TAIL - j * 128)
        turned = tail[:, j * 128 : (j + 1) * 128].T.astype(bf16)
        tokens_ref[OUT_W + j * 128 : OUT_W + j * 128 + high_row, :] = turned[0:high_row]


def combine(ids, logits, wire):
    return pl.pallas_call(
        combine_kernel,
        out_shape=(jax.ShapeDtypeStruct((D, TOK), bf16), jax.ShapeDtypeStruct((TOP, TOK), f32)),
        compiler_params=pltpu.CompilerParams(vmem_limit_bytes=20 * MB),
        cost_estimate=pl.CostEstimate(flops=2 * 512 * 1024 * OUT_W, bytes_accessed=5 * MB, transcendentals=512),
        name="combine",
    )(ids, logits, wire)


def exchange(wire):
    rows, width = wire.shape
    cut = wire.reshape(EXP, ROWS, width)
    return lax.all_to_all(cut, ("seq", "head"), split_axis=0, concat_axis=0, tiled=True).reshape(rows, width)


def body(tokens, grad_out, expert_ids, router_logits, w_gate, w_up, w_down):
    ids = expert_ids.T
    there = exchange(dispatch(ids, tokens.T, grad_out.T))
    back = exchange(experts(there, w_gate[0].T, w_up[0].T, w_down[0]))
    grad_tokens, grad_logits = combine(ids, router_logits.T, back)
    return grad_tokens.T, grad_logits.T


def solution(mesh):
    rows = P(("seq", "head"), None)
    slabs = P(("seq", "head"), None, None)
    return jax.shard_map(
        body,
        mesh=mesh,
        in_specs=(rows, rows, rows, rows, slabs, slabs, slabs),
        out_specs=(rows, rows),
        check_vma=False,
    )
```

```python
import jax
import jax.numpy as jnp
from jax import lax
from jax.experimental import pallas as pl
from jax.experimental.pallas import tpu as pltpu
from jax.sharding import PartitionSpec as P

swish_scale = 1.702

D = 2880
FF = 1440
TOP = 4
TOK = 128
EXP = 128
CAP = 5
ROWS = 8
EXTRA = 2944
PIECE = 768
IN_W = EXTRA + PIECE
OUT_W = 1920
TAIL = D - OUT_W
RIGHT = 1024
SCORE_AT = 1280
GROUP = 32
PAIRS = GROUP * CAP
GROUPS = TOK // GROUP


def parts_of(total, width):
    return [(start, min(width, total - start)) for start in range(0, total, width)]


F_PARTS = parts_of(FF, 256)
D_PARTS = parts_of(D, 512)
VMEM_MB = 26
P_PARTS = parts_of(D, PIECE)
SEND_STEPS, SEND_MB = 4, 24
MB = 1024 * 1024
bf16 = jnp.bfloat16
f32 = jnp.float32


def iota(shape, dim):
    return lax.broadcasted_iota(jnp.int32, shape, dim)


def as_bf16(mask):
    return jnp.where(mask, 1.0, 0.0).astype(bf16)


def dot_nt(a, b):
    return lax.dot_general(a, b, (((1,), (1,)), ((), ())), preferred_element_type=f32)


def dot_nn(a, b):
    return jnp.dot(a, b, preferred_element_type=f32)


def ranks_of(ids):
    expert = iota((EXP, TOK), 0)
    naming = ids[0:1, :] == expert
    for k in range(1, TOP):
        naming = jnp.logical_or(naming, ids[k : k + 1, :] == expert)
    before = as_bf16(iota((TOK, TOK), 0) < iota((TOK, TOK), 1))
    rank = dot_nn(as_bf16(naming), before)
    return naming, jnp.where(naming, rank, -1.0)


def dispatch_kernel(ids_ref, x_hbm, dy_hbm, out_hbm, both, pieces, parts, in_sem, out_sem):
    sources = [(x_hbm, both.at[:, 0:TOK]), (dy_hbm, both.at[:, TOK : 2 * TOK])]
    for c, (start, width) in enumerate(P_PARTS):
        lanes = slice(c * TOK, (c + 1) * TOK)
        sources.append((dy_hbm.at[start : start + width, :], pieces.at[0:width, lanes]))
        if width < PIECE:
            pieces[width:PIECE, lanes] = jnp.zeros((PIECE - width, TOK), bf16)
    fetches = [pltpu.make_async_copy(source, to, in_sem.at[n]) for n, (source, to) in enumerate(sources)]
    for fetch in fetches:
        fetch.start()

    _, rank = ranks_of(ids_ref[...])
    rank = rank.astype(bf16)
    rows = EXP // SEND_STEPS * ROWS
    q = iota((rows, TOK), 0) & 7
    picks = []
    for n in range(SEND_STEPS):
        spread = as_bf16(iota((rows, EXP), 1) == n * (rows // ROWS) + (iota((rows, EXP), 0) >> 3))
        slot = dot_nn(spread, rank).astype(jnp.int32)
        front = [jnp.logical_and(slot == q, q < CAP), jnp.logical_and(slot == q - CAP, q >= CAP)]
        late = slot == 3 + (q >> 2)
        rest = [jnp.logical_and(late, (q & 3) == c) for c in range(4)]
        picks.append([jnp.concatenate([as_bf16(m) for m in masks], axis=1) for masks in (front, rest)])
        parts[n, :, D:EXTRA] = jnp.zeros((rows, EXTRA - D), bf16)
    for fetch in fetches:
        fetch.wait()
    sends = []
    for n, (front, rest) in enumerate(picks):
        parts[n, :, 0:D] = dot_nt(front, both[...]).astype(bf16)
        parts[n, :, EXTRA:IN_W] = dot_nt(rest, pieces[...]).astype(bf16)
        sends.append(pltpu.make_async_copy(parts.at[n], out_hbm.at[n * rows : (n + 1) * rows, :], out_sem.at[n]))
        sends[n].start()
    for send in sends:
        send.wait()


def dispatch(ids, x, dy):
    anywhere = pl.BlockSpec(memory_space=pl.ANY)
    operands = [pltpu.with_memory_space_constraint(v, pltpu.HBM) for v in (ids, x, dy)]
    return pl.pallas_call(
        dispatch_kernel,
        out_shape=pltpu.HBM((EXP * ROWS, IN_W), bf16),
        in_specs=[pl.BlockSpec(memory_space=pltpu.VMEM), anywhere, anywhere],
        out_specs=anywhere,
        scratch_shapes=[
            pltpu.VMEM((D, 2 * TOK), bf16),
            pltpu.VMEM((PIECE, 4 * TOK), bf16),
            pltpu.VMEM((SEND_STEPS, EXP // SEND_STEPS * ROWS, IN_W), bf16),
            pltpu.SemaphoreType.DMA((2 + len(P_PARTS),)),
            pltpu.SemaphoreType.DMA((SEND_STEPS,)),
        ],
        compiler_params=pltpu.CompilerParams(vmem_limit_bytes=SEND_MB * MB),
        cost_estimate=pl.CostEstimate(flops=8 * 1024 * 256 * 4400, bytes_accessed=40 * MB, transcendentals=0),
        name="dispatch",
    )(*operands)


def place(slot, block):
    tail = block - OUT_W // 128
    if tail < 0:
        return slot, block
    if slot % 2 == 0:
        return CAP + slot // 2, tail
    if tail < 7:
        return CAP + slot // 2, RIGHT // 128 + tail
    return 7, RIGHT // 128 + slot // 2


def expert_kernel(wire, gate_w, up_w, down_w, out_ref, x_all, dy_all, d_gate, d_up, wide):
    rows = GROUP * ROWS
    r, c = iota((rows, rows), 0), iota((rows, rows), 1)
    main = as_bf16(c == (r & 31) * ROWS + (r >> 5))
    late = as_bf16(c == (r & 31) * ROWS + ((r >> 5) & 1) * 4 + (r >> 6))
    for g in range(GROUPS):
        to = g * PAIRS
        at = slice(g * rows, (g + 1) * rows)
        front = dot_nn(main, wire[at, 0:D]).astype(bf16)
        x_all[to : to + PAIRS, :] = front[0:PAIRS]
        dy_all[to : to + 96, :] = front[PAIRS:rows]
        rest = dot_nn(late, wire[at, EXTRA:IN_W]).astype(bf16)
        for p in range(4):
            high = min(PIECE, D - p * PIECE)
            dy_all[to + 96 : to + PAIRS, p * PIECE : p * PIECE + high] = rest[p * 64 : (p + 1) * 64, 0:high]

    score = jnp.zeros((GROUPS * PAIRS, 1), f32)
    held = None
    for j in range(len(F_PARTS) + 1):
        fresh = None
        if j < len(F_PARTS):
            start, width = F_PARTS[j]
            units = slice(start, start + width)
            fresh = (
                units,
                dot_nt(x_all[...], gate_w[units, :]),
                dot_nt(x_all[...], up_w[units, :]),
                dot_nt(dy_all[...], down_w[units, :]),
            )
        if held is not None:
            units, gate, up, back = held
            sig = jax.nn.sigmoid(swish_scale * gate)
            act = gate * sig
            back_up = back * (up + 1.0)
            score = score + jnp.sum(act * back_up, axis=1, keepdims=True)
            d_gate[:, units] = (back_up * (sig + swish_scale * act * (1.0 - sig))).astype(bf16)
            d_up[:, units] = (back * act).astype(bf16)
        held = fresh

    half = 2 * rows
    for h in range(2):
        own = slice(2 * h * PAIRS, 2 * (h + 1) * PAIRS)
        for start, width in D_PARTS:
            columns = slice(start, start + width)
            grad = dot_nn(d_gate[own, :], gate_w[:, columns]) + dot_nn(d_up[own, :], up_w[:, columns])
            if width % 128:
                grad = jnp.concatenate([grad, jnp.zeros((2 * PAIRS, 64), f32)], axis=1)
            for g in range(2):
                for s in range(CAP):
                    at = g * PAIRS + s * GROUP
                    for n in range(0, width, 128):
                        q, to = place(s, (start + n) // 128)
                        block = grad[at : at + GROUP, n : n + 128]
                        wide[to, pl.ds(g * rows + q, GROUP, stride=ROWS), :] = block
        for g in range(2):
            for s in range(CAP):
                at = (2 * h + g) * PAIRS + s * GROUP
                wide[SCORE_AT // 128 + s, pl.ds(g * rows + 7, GROUP, stride=ROWS), :] = jnp.broadcast_to(
                    score[at : at + GROUP], (GROUP, 128)
                )
        for n in range(OUT_W // 128):
            out_ref[h * half : (h + 1) * half, n * 128 : (n + 1) * 128] = wide[n, 0:half, :].astype(bf16)


def experts(wire, gate_w, up_w, down_w):
    near = pl.BlockSpec(memory_space=pltpu.VMEM)
    operands = [pltpu.with_memory_space_constraint(v, pltpu.VMEM) for v in (wire, gate_w, up_w, down_w)]
    return pl.pallas_call(
        expert_kernel,
        out_shape=pltpu.VMEM((TOK * ROWS, OUT_W), bf16),
        in_specs=[near] * 4,
        out_specs=near,
        scratch_shapes=[
            pltpu.VMEM((GROUPS * PAIRS, D), bf16),
            pltpu.VMEM((GROUPS * PAIRS, D), bf16),
            pltpu.VMEM((GROUPS * PAIRS, FF), bf16),
            pltpu.VMEM((GROUPS * PAIRS, FF), bf16),
            pltpu.VMEM((OUT_W // 128, 2 * GROUP * ROWS + ROWS, 128), f32),
        ],
        compiler_params=pltpu.CompilerParams(vmem_limit_bytes=VMEM_MB * MB),
        cost_estimate=pl.CostEstimate(flops=2 * 640 * 5 * D * FF, bytes_accessed=37 * MB, transcendentals=640 * FF),
        name="experts",
    )(*operands)


def combine_kernel(ids_ref, logits_ref, wire_ref, tokens_ref, logits_out_ref):
    ids = ids_ref[...]
    logits = logits_ref[...]
    scaled = jnp.exp(logits - jnp.max(logits, axis=0, keepdims=True))
    weights = scaled / jnp.sum(scaled, axis=0, keepdims=True)
    naming, rank = ranks_of(ids)
    expert = iota((EXP, TOK), 0)
    spread_w = jnp.zeros((EXP, TOK), f32)
    for k in range(TOP):
        spread_w = spread_w + jnp.where(ids[k : k + 1, :] == expert, weights[k : k + 1, :], 0.0)

    all_rows = TOK * ROWS
    sevenths = as_bf16(iota((EXP, all_rows), 1) == iota((EXP, all_rows), 0) * ROWS + 7)
    marks = dot_nn(sevenths, wire_ref[:, SCORE_AT:OUT_W])
    score_of = jnp.zeros((EXP, TOK), f32)
    for s in range(CAP):
        score_of = score_of + jnp.where(rank == float(s), marks[:, 128 * s : 128 * s + 1], 0.0)
    scores = [
        jnp.sum(jnp.where(ids[k : k + 1, :] == expert, score_of, 0.0), axis=0, keepdims=True) for k in range(TOP)
    ]
    mean = sum(weights[k : k + 1, :] * scores[k] for k in range(TOP))
    for k in range(TOP):
        logits_out_ref[k : k + 1, :] = weights[k : k + 1, :] * (scores[k] - mean)

    spread = as_bf16(iota((EXP, all_rows), 0) == iota((EXP, all_rows), 1) >> 3)
    wide = dot_nn(jnp.concatenate([spread_w.T, rank.T], axis=0).astype(bf16), spread)
    weight = wide[0:TOK].astype(bf16)
    slot = wide[TOK : 2 * TOK].astype(jnp.int32)
    q = iota((TOK, all_rows), 1) & 7
    late = q >= CAP

    def picked(mask):
        return jnp.where(mask, weight, jnp.zeros((), bf16))

    main = picked(slot == q)
    left = picked(jnp.logical_and(late, slot == 2 * (q - CAP)))
    right = picked(jnp.logical_and(late, slot == 2 * (q - CAP) + 1))
    ends = [
        dot_nn(picked(jnp.logical_and(q == 7, slot == 2 * i + 1)), wire_ref[:, RIGHT + 128 * i : RIGHT + 128 * (i + 1)])
        for i in range(2)
    ]
    a = dot_nn(jnp.concatenate([main, left], axis=0), wire_ref[:, 0:RIGHT])
    b = dot_nn(jnp.concatenate([main, right], axis=0), wire_ref[:, RIGHT:OUT_W])
    front = jnp.concatenate([a[0:TOK], b[0:TOK]], axis=1)
    tail = a[TOK : 2 * TOK] + jnp.concatenate([b[TOK : 2 * TOK], ends[0] + ends[1]], axis=1)
    for j in range(OUT_W // 128):
        tokens_ref[j * 128 : (j + 1) * 128, :] = front[:, j * 128 : (j + 1) * 128].T.astype(bf16)
    for j in range(8):
        high_row = min(128, TAIL - j * 128)
        turned = tail[:, j * 128 : (j + 1) * 128].T.astype(bf16)
        tokens_ref[OUT_W + j * 128 : OUT_W + j * 128 + high_row, :] = turned[0:high_row]


def combine(ids, logits, wire):
    return pl.pallas_call(
        combine_kernel,
        out_shape=(jax.ShapeDtypeStruct((D, TOK), bf16), jax.ShapeDtypeStruct((TOP, TOK), f32)),
        compiler_params=pltpu.CompilerParams(vmem_limit_bytes=20 * MB),
        cost_estimate=pl.CostEstimate(flops=2 * 512 * 1024 * OUT_W, bytes_accessed=5 * MB, transcendentals=512),
        name="combine",
    )(ids, logits, wire)


def exchange(wire):
    rows, width = wire.shape
    cut = wire.reshape(EXP, ROWS, width)
    return lax.all_to_all(cut, ("seq", "head"), split_axis=0, concat_axis=0, tiled=True).reshape(rows, width)


def body(tokens, grad_out, expert_ids, router_logits, w_gate, w_up, w_down):
    ids = expert_ids.T
    there = exchange(dispatch(ids, tokens.T, grad_out.T))
    back = exchange(experts(there, w_gate[0].T, w_up[0].T, w_down[0]))
    grad_tokens, grad_logits = combine(ids, router_logits.T, back)
    return grad_tokens.T, grad_logits.T


def solution(mesh):
    rows = P(("seq", "head"), None)
    slabs = P(("seq", "head"), None, None)
    return jax.shard_map(
        body,
        mesh=mesh,
        in_specs=(rows, rows, rows, rows, slabs, slabs, slabs),
        out_specs=(rows, rows),
        check_vma=False,
    )
```
